32 devices in a mesh: ep: 8 (over z, x), dp: 4 (over y, core).
Axes of the slice: x: 2, y: 2, z: 4, core: 2. Of those that a mesh axis runs over, the one named last changes fastest.
Arguments:
- tokens: bfloat16 [2048, 2048], P(('dp', 'ep')), parts along dimension 0, may hold values from -6 to 6
- gates: float32 [2048, 2], P(('dp', 'ep')), parts along dimension 0, may hold values from 0.05 to 1
- expert_ids: int32 [2048, 2], P(('dp', 'ep')), parts along dimension 0, may hold values from 0 to 1, all different within a row; in each aligned block of 64 rows (0 to 63, 64 to 127, ...) at most 64 rows name the same one
- slot_expert: int32 [8], P('dp'), parts along dimension 0, may hold values from 0 to 1, each once
- w_in: bfloat16 [32, 2, 192, 2048], P(('dp', 'ep')), parts along dimension 0, may hold values from -0.125 to 0.125
- w_out: bfloat16 [32, 192, 2048], P(('dp', 'ep')), parts along dimension 0, may hold values from -0.21875 to 0.21875
Outputs:
- mixed: bfloat16 [2048, 2048], P(('dp', 'ep')), parts along dimension 0
The draws below stay inside these ranges and needn't reach their ends.
There are 4 independent parts, one for each index of `dp`. The reference program is written for one: setup_inputs(seed, part) draws one part's arguments, and reference() takes and returns one part's arrays. A program takes and returns all parts, laid end to end along the dimension named above; each array names one. Nothing has to cross between parts.
All inputs are finite; a program needn't handle non-finite values.
Results may differ from the reference program's by a relative error of at most 0.0058.
Values may be sent and summed in bfloat16 or wider, within the bound.
No kernel may reach another device: no remote copies, remote signals or barrier semaphores. Data moves between devices by JAX's collectives and lax.ppermute only.
A program may use at most 64 MiB of HBM per device.

```python
import math
import jax
import jax.numpy as jnp
import numpy as np
from jax import lax

D = 2048
FF = 768
GROUP = 4
TOK_DEV = 64
FF_DEV = 192
EXPERTS = 2
TOP = 2
TOKENS = 512
CAPE = 64
N_EP = 8


def block_levels(rng, dims, shards, smallest, largest):
    gain = 1.0
    for dim, shards_of in shards:
        steps = jax.random.uniform(jax.random.fold_in(jax.random.fold_in(rng, 6), dim), (shards_of,), jnp.float32, smallest / len(shards), largest / len(shards))
        gain = gain * jnp.repeat(jnp.exp(steps), dims[dim] // shards_of).reshape((-1,) + (1,) * (len(dims) - 1 - dim))
    return gain


def routed_block(stream_key, own, number, rows, number_of, top, most, lean):
    ranking = jax.random.permutation(stream_key, number_of)
    heavy_load, ordinary = portions_of(number_of, rows * top, most, lean, True), portions_of(number_of, rows * top, most, lean, False)
    places = jnp.arange(number_of)

    def named(lengths, rotation):
        used = int((lengths > 0).sum())
        fixed = max(1, used // 4)
        shifted = fixed + (places - fixed + rotation * (used - fixed)) % max(1, number_of - fixed)
        return jnp.zeros((number_of,), jnp.int32).at[ranking[jnp.where(places < fixed, places, shifted)]].set(jnp.asarray(lengths, jnp.int32))

    lengths = jnp.where(number % 4 == 0, named(heavy_load, number // 4), named(ordinary, number - number // 4 - 1))
    mixed = jax.random.permutation(jax.random.fold_in(own, 3), number_of)
    source_of, sink = mixed[0:number_of // 2 * 2:2], mixed[1:number_of // 2 * 2:2]
    margin = jnp.minimum(lengths[source_of] - 1, most - lengths[sink]) // 2
    margin = jnp.where((source_of == ranking[0]) | (sink == ranking[0]) | (lengths[sink] == 0), 0, jnp.maximum(margin, 0))
    shifted = jax.random.randint(jax.random.fold_in(own, 4), (number_of // 2,), 0, 1 << 20) % (margin + 1)
    lengths = lengths.at[source_of].add(-shifted).at[sink].add(shifted)
    items = jnp.searchsorted(jnp.cumsum(lengths), jnp.arange(rows * top), side="right").astype(jnp.int32)
    table = items.reshape(top, rows).T
    table = table[jax.random.permutation(jax.random.fold_in(own, 1), rows)]
    rotation = jax.random.randint(jax.random.fold_in(own, 2), (rows, 1), 0, top)
    return jnp.take_along_axis(table, (jnp.arange(top)[None, :] + rotation) % top, axis=1)


def portions_of(count, total, most, lean, full):
    weights = [(1 << 20) // math.isqrt(standing ** lean) + 1 for standing in range(1, count + 1)]
    largest = most if full else min(most, max(-(-total // count), total * weights[0] // sum(weights)))
    least = 1 if total - largest >= count - 1 else 0
    holding, spare = [largest] + [least] * (count - 1), total - largest - least * (count - 1)
    while spare > 0:
        free = [i for i in range(1, count) if holding[i] < largest] or [i for i in range(1, count) if holding[i] < most]
        pool, budget = sum([weights[i] for i in free]), spare
        for i in free:
            more = min(most - holding[i], max(1, budget * weights[i] // pool), spare)
            holding[i] = holding[i] + more
            spare = spare - more
    return np.array(holding)


def bell_draw(rng, dims, scale, most, pieces=(), kind=jnp.bfloat16):
    values = scale * jax.random.normal(rng, dims, jnp.float32)
    if pieces:
        values = values * block_levels(rng, dims, pieces, -0.22, 0.18)
    return jnp.clip(values, -most, most).astype(kind)


def setup_inputs(seed: int = 0, part: int = 0) -> dict:
    keys = jax.random.split(jax.random.key(seed), 7)
    part_keys = jax.random.split(jax.random.fold_in(keys[6], part), 7)
    tokens = bell_draw(part_keys[0], (TOKENS, D), 1.0, 6.0, ((0, 8),))
    gates = jnp.clip(jnp.exp(math.log(1.0) - 2.9957323 * jax.random.uniform(part_keys[1], (TOKENS, TOP), jnp.float32) ** block_levels(part_keys[1], (TOKENS, TOP), ((0, 8),), -0.2, 0.2)), 0.05, 1.0)
    expert_ids_keys = jax.random.split(jax.random.fold_in(part_keys[2], 1), TOKENS // TOK_DEV)
    expert_ids_turns = jax.random.permutation(jax.random.fold_in(part_keys[2], 3), TOKENS // TOK_DEV)
    expert_ids = jax.vmap(lambda own, number: routed_block(jax.random.fold_in(part_keys[2], 2), own, number, TOK_DEV, EXPERTS, TOP, CAPE, 2))(expert_ids_keys, expert_ids_turns).reshape((TOKENS, TOP))
    slot_expert = jax.random.permutation(part_keys[3], EXPERTS).astype(jnp.int32)
    w_in = bell_draw(part_keys[4], (N_EP, 2, FF_DEV, D), D ** -0.5, 0.125, ((0, 8),))
    w_out = bell_draw(part_keys[5], (N_EP, FF_DEV, D), FF ** -0.5, 0.21875, ((0, 8),))
    return {"tokens": tokens, "gates": gates, "expert_ids": expert_ids, "slot_expert": slot_expert, "w_in": w_in, "w_out": w_out}


def reference(tokens, gates, expert_ids, slot_expert, w_in, w_out):
    expert_range = jnp.arange(EXPERTS, dtype=jnp.int32)
    home = jnp.zeros((EXPERTS,), jnp.int32).at[slot_expert].set(expert_range)
    flat_ids = expert_ids.reshape(-1)
    order = jnp.argsort(flat_ids, stable=True).astype(jnp.int32)
    counts = jnp.sum((flat_ids[:, None] == expert_range[None, :]).astype(jnp.int32), axis=0)
    starts = (jnp.cumsum(counts) - counts).astype(jnp.int32)
    limit = N_EP * CAPE
    padded = jnp.concatenate([order, jnp.zeros((limit,), jnp.int32)])
    gate_flat = gates.reshape(-1)

    def visit(total, expert):
        index_rows = lax.dynamic_slice(padded, (starts[expert].astype(jnp.int32),), (limit,))
        valid = jnp.arange(limit, dtype=jnp.int32) < counts[expert]
        source_token = index_rows // TOP
        chosen = tokens[source_token].astype(jnp.float32)
        first = (home[expert] * GROUP).astype(jnp.int32)
        weights_in = lax.dynamic_slice_in_dim(w_in, first, GROUP, 0).astype(jnp.float32)
        weights_out = lax.dynamic_slice_in_dim(w_out, first, GROUP, 0).astype(jnp.float32)
        gate_part = jnp.einsum("rd,jfd->rjf", chosen, weights_in[:, 0])
        up_part = jnp.einsum("rd,jfd->rjf", chosen, weights_in[:, 1])
        hidden = (jax.nn.silu(gate_part) * up_part).astype(jnp.bfloat16)
        result = jnp.einsum("rjf,jfd->rd", hidden.astype(jnp.float32), weights_out).astype(jnp.bfloat16)
        weight = jnp.where(valid, gate_flat[index_rows], jnp.zeros((), gate_flat.dtype))
        total = total.at[source_token].add(weight[:, None].astype(jnp.float32) * result.astype(jnp.float32))
        return total, None

    total, unused = lax.scan(visit, jnp.zeros((TOKENS, D), jnp.float32), expert_range)
    return total.astype(jnp.bfloat16)
```

```python
import functools

import jax
import jax.numpy as jnp
from jax import lax
from jax.experimental import pallas as pl
from jax.experimental.pallas import tpu as pltpu
from jax.sharding import PartitionSpec as P

GROUP = 4
BLOCK = 128


def from_partner(block, axis, apart):
    count = lax.axis_size(axis)
    route = []
    for low in range(count):
        high = low | 1 << apart
        if high != low and high < count:
            route += [(low, high), (high, low)]
    return lax.ppermute(block, axis, route)


def from_member(block, apart):
    count = lax.axis_size("ep")
    return lax.ppermute(block, "ep", [(i, i ^ apart) for i in range(count)])


def from_group(block, steps):
    count = lax.axis_size("ep")
    return lax.ppermute(block, "ep", [(i, (i - steps * GROUP) % count) for i in range(count)])


def share_kernel(*refs):
    n = (len(refs) - 2) // 2
    w_in, w_out = refs[n], refs[n + 1]
    rows = refs[0].shape[0]
    x = jnp.concatenate([r[...] for r in refs[:n]], axis=0)
    contract = (((1,), (1,)), ((), ()))
    gate = lax.dot_general(x, w_in[0, 0], contract, preferred_element_type=jnp.float32)
    up = lax.dot_general(x, w_in[0, 1], contract, preferred_element_type=jnp.float32)
    hidden = (gate / (1.0 + jnp.exp(-gate)) * up).astype(jnp.bfloat16)
    for i in range(n):
        refs[n + 2 + i][...] = jnp.dot(
            hidden[i * rows : (i + 1) * rows], w_out[0], preferred_element_type=jnp.float32
        ).astype(jnp.bfloat16)


def share(blocks, w_in, w_out):
    rows, width = blocks[0].shape
    units = w_out.shape[1]
    n = len(blocks)
    return pl.pallas_call(
        share_kernel,
        out_shape=[jax.ShapeDtypeStruct((rows, width), jnp.bfloat16)] * n,
        in_specs=[pl.BlockSpec(memory_space=pltpu.VMEM)] * (n + 2),
        out_specs=[pl.BlockSpec(memory_space=pltpu.VMEM)] * n,
        compiler_params=pltpu.CompilerParams(vmem_limit_bytes=32 << 20),
        cost_estimate=pl.CostEstimate(
            flops=6 * n * rows * width * units,
            bytes_accessed=2 * (2 * n * rows * width + 3 * units * width),
            transcendentals=n * rows * units,
        ),
        name="share",
    )(*blocks, w_in, w_out)


def everywhere(tokens, gates, expert_ids, slot_expert, w_in, w_out):
    experts = lax.axis_size("ep") // GROUP
    my_group = lax.axis_index("ep") // GROUP
    visitors = [from_group(tokens, s) for s in range(1, experts)]
    held = [[tokens] + [from_member(tokens, m) for m in range(1, GROUP)]]
    for rows in visitors:
        held.append([rows] + [from_member(rows, m) for m in range(1, GROUP)])
    sums = []
    for blocks in held:
        shares = share(blocks, w_in, w_out)
        total = shares[0].astype(jnp.float32)
        for m in range(1, GROUP):
            total = total + from_member(shares[m], m).astype(jnp.float32)
        sums.append(total.astype(jnp.bfloat16))
    mixed = jnp.zeros(tokens.shape, jnp.float32)
    for s in range(experts):
        rows = sums[0] if s == 0 else from_group(sums[s], experts - s)
        source = (my_group + (experts - s if s else 0)) % experts
        named = lax.dynamic_index_in_dim(slot_expert, source, 0, keepdims=False)
        weight = jnp.sum(jnp.where(expert_ids == named, gates, 0.0), axis=1, keepdims=True)
        mixed = mixed + weight * rows.astype(jnp.float32)
    return mixed.astype(jnp.bfloat16)


def routed(tokens, gates, expert_ids, slot_expert, w_in, w_out):
    members = lax.axis_size("ep")
    myself = lax.axis_index("ep")
    tok_rows, width = tokens.shape
    top_count = expert_ids.shape[1]
    experts = members // GROUP
    cap_expert = min(tok_rows, 5 * tok_rows * top_count // (4 * experts))
    cap_member = (cap_expert + GROUP - 1) // GROUP
    slot_total = members * cap_member
    block_limit = slot_total // BLOCK + 1
    expert_range = jnp.arange(experts, dtype=jnp.int32)
    home = jnp.sum(
        jnp.where(slot_expert[:, None] == expert_range[None, :], expert_range[:, None], 0), axis=0
    )
    pieces_in, pieces_out = (w_in, w_out)
    bit_order = (0, 1)
    for swap_bit in bit_order:
        other_in, other_out = from_partner((pieces_in, pieces_out), "ep", swap_bit)
        lower = myself // (1 << swap_bit) % 2 == 0
        pieces_in = jnp.where(
            lower,
            jnp.concatenate([pieces_in, other_in], axis=0),
            jnp.concatenate([other_in, pieces_in], axis=0),
        )
        pieces_out = jnp.where(
            lower,
            jnp.concatenate([pieces_out, other_out], axis=0),
            jnp.concatenate([other_out, pieces_out], axis=0),
        )
    flat_ids = expert_ids.reshape(-1)
    onehot = (flat_ids[:, None] == expert_range[None, :]).astype(jnp.int32)
    rank = jnp.sum(jnp.cumsum(onehot, axis=0) * onehot, axis=1) - 1
    group = jnp.sum(onehot * home[None, :], axis=1)
    member = rank // cap_member
    slot = rank % cap_member
    slot_index = (group * GROUP + member) * cap_member + slot
    repeated = jnp.repeat(tokens, top_count, axis=0)
    send_rows = jnp.zeros((slot_total, width), jnp.bfloat16).at[slot_index].set(repeated)
    send_flag = (
        jnp.zeros((slot_total,), jnp.bfloat16).at[slot_index].set(jnp.ones((), jnp.bfloat16))
    )
    recv_rows, recv_flag = (
        lax.all_to_all(send_rows, "ep", split_axis=0, concat_axis=0, tiled=True),
        lax.all_to_all(send_flag, "ep", split_axis=0, concat_axis=0, tiled=True),
    )
    valid = recv_flag > 0.5
    valid_count = jnp.sum(valid.astype(jnp.int32))
    blocks_total = (valid_count + BLOCK - 1) // BLOCK
    position = jnp.where(valid, jnp.cumsum(valid.astype(jnp.int32)) - 1, block_limit * BLOCK)
    compact = (
        jnp.zeros((block_limit * BLOCK, width), jnp.bfloat16)
        .at[position]
        .set(recv_rows, mode="drop")
    )
    gate_weights = pieces_in[:, 0]
    up_weights = pieces_in[:, 1]

    def compute_block(block, result):
        block_rows = lax.dynamic_slice_in_dim(compact, block * BLOCK, BLOCK, 0)
        gate_part = jnp.einsum(
            "rd,jfd->rjf", block_rows, gate_weights, preferred_element_type=jnp.float32
        )
        up_part = jnp.einsum(
            "rd,jfd->rjf", block_rows, up_weights, preferred_element_type=jnp.float32
        )
        hidden = (jax.nn.silu(gate_part) * up_part).astype(jnp.bfloat16)
        produced = jnp.einsum(
            "rjf,jfd->rd", hidden, pieces_out, preferred_element_type=jnp.float32
        ).astype(jnp.bfloat16)
        return lax.dynamic_update_slice_in_dim(result, produced, block * BLOCK, 0)

    computed = lax.fori_loop(
        0, blocks_total, compute_block, jnp.zeros((block_limit * BLOCK, width), jnp.bfloat16)
    )
    back_rows = jnp.where(
        valid[:, None],
        computed[jnp.minimum(position, block_limit * BLOCK - 1)],
        jnp.zeros((), jnp.bfloat16),
    )
    returned = lax.all_to_all(back_rows, "ep", split_axis=0, concat_axis=0, tiled=True)
    gathered = returned[slot_index].reshape(tok_rows, top_count, width)
    total = jnp.zeros((tok_rows, width), jnp.float32)
    for choice_index in range(top_count):
        total = total + gates[:, choice_index][:, None] * gathered[:, choice_index].astype(
            jnp.float32
        )
    return total.astype(jnp.bfloat16)


def local(tokens, gates, expert_ids, slot_expert, w_in, w_out):
    plan = everywhere if expert_ids.shape[1] == slot_expert.shape[0] else routed
    return plan(tokens, gates, expert_ids, slot_expert, w_in, w_out)


def solution(mesh):
    return jax.shard_map(
        local,
        mesh=mesh,
        in_specs=(
            P(("dp", "ep"), None),
            P(("dp", "ep"), None),
            P(("dp", "ep"), None),
            P("dp"),
            P(("dp", "ep"), None, None, None),
            P(("dp", "ep"), None, None),
        ),
        out_specs=P(("dp", "ep"), None),
        check_vma=False,
    )
```

```python
import jax
import jax.numpy as jnp
from jax import lax
from jax.experimental import pallas as pl
from jax.experimental.pallas import tpu as pltpu
from jax.sharding import PartitionSpec as P

GROUP = 4
BLOCK = 128


def from_partner(block, axis, apart):
    count = lax.axis_size(axis)
    route = []
    for low in range(count):
        high = low | 1 << apart
        if high != low and high < count:
            route += [(low, high), (high, low)]
    return lax.ppermute(block, axis, route)


def exchange(block, *apart):
    replicas, count = lax.axis_size("dp"), lax.axis_size("ep")
    route = []
    for d in range(replicas):
        bits = apart[d % len(apart)]
        route += [(i * replicas + d, (i ^ bits) * replicas + d) for i in range(count)]
    return lax.ppermute(block, ("ep", "dp"), route)


def after(value, *others):
    return lax.optimization_barrier((value, *others))[0]


def touch_kernel(w_in, w_out, out):
    out[...] = w_in[0, 0, :8, :128] + w_out[0, :8, :128]


def touch(w_in, w_out):
    return pl.pallas_call(
        touch_kernel,
        out_shape=jax.ShapeDtypeStruct((8, 128), jnp.bfloat16),
        in_specs=[pl.BlockSpec(memory_space=pltpu.VMEM)] * 2,
        out_specs=pl.BlockSpec(memory_space=pltpu.VMEM),
        compiler_params=pltpu.CompilerParams(has_side_effects=True),
        name="touch",
    )(w_in, w_out)


def share_kernel(*refs):
    n = (len(refs) - 2) // 2
    w_in, w_out = refs[n], refs[n + 1]
    rows = refs[0].shape[0]
    x = jnp.concatenate([r[...] for r in refs[:n]], axis=0)
    contract = (((1,), (1,)), ((), ()))
    gate = lax.dot_general(x, w_in[0, 0], contract, preferred_element_type=jnp.float32)
    up = lax.dot_general(x, w_in[0, 1], contract, preferred_element_type=jnp.float32)
    hidden = (gate / (1.0 + jnp.exp(-gate)) * up).astype(jnp.bfloat16)
    for i in range(n):
        refs[n + 2 + i][...] = jnp.dot(
            hidden[i * rows : (i + 1) * rows], w_out[0], preferred_element_type=jnp.float32
        ).astype(jnp.bfloat16)


def share(blocks, w_in, w_out):
    rows, width = blocks[0].shape
    units = w_out.shape[1]
    n = len(blocks)
    return pl.pallas_call(
        share_kernel,
        out_shape=[jax.ShapeDtypeStruct((rows, width), jnp.bfloat16)] * n,
        in_specs=[pl.BlockSpec(memory_space=pltpu.VMEM)] * (n + 2),
        out_specs=[pl.BlockSpec(memory_space=pltpu.VMEM)] * n,
        compiler_params=pltpu.CompilerParams(vmem_limit_bytes=32 << 20),
        cost_estimate=pl.CostEstimate(
            flops=6 * n * rows * width * units,
            bytes_accessed=2 * (2 * n * rows * width + 3 * units * width),
            transcendentals=n * rows * units,
        ),
        name="share",
    )(*blocks, w_in, w_out)


def summed(*shares):
    total = shares[0].astype(jnp.float32)
    for s in shares[1:]:
        total = total + s.astype(jnp.float32)
    return total.astype(jnp.bfloat16)


def everywhere(tokens, gates, expert_ids, slot_expert, w_in, w_out):
    first, second, across, group = (1, 2), (2, 1), (3, 3), (4, 4)
    my_group = lax.axis_index("ep") // GROUP
    weights = []
    for s in range(2):
        named = lax.dynamic_index_in_dim(slot_expert, (my_group + s) % 2, 0, keepdims=False)
        weights.append(jnp.sum(jnp.where(expert_ids == named, gates, 0.0), axis=1, keepdims=True))
    theirs = exchange(tokens, *group)
    ours_a = exchange(tokens, *first)
    ours_b = exchange(tokens, *second)
    ours_d = exchange(ours_a, *second)
    theirs = after(theirs, touch(w_in, w_out), ours_a, ours_b, ours_d)
    theirs_a = exchange(theirs, *first)
    theirs_b = exchange(theirs, *second)
    theirs_d = exchange(theirs, *across)
    away = share([theirs, theirs_a, theirs_b, theirs_d], w_in, w_out)
    away_d = exchange(away[3], *across)
    away_a = exchange(away[1], *first)
    away_b = exchange(away[2], *second)
    home = share([after(tokens, away[0]), ours_a, ours_b, ours_d], w_in, w_out)
    away_sum = summed(away[0], away_d, away_a, away_b)
    other = exchange(away_sum, *group)
    home = [after(h, away_d) for h in home]
    home_d = exchange(home[3], *first)
    home_a = exchange(home[1], *first)
    home_b = exchange(summed(home[2], home_d), *second)
    own = summed(home[0], home_a, home_b)
    return (
        weights[0] * own.astype(jnp.float32) + weights[1] * other.astype(jnp.float32)
    ).astype(jnp.bfloat16)


def routed(tokens, gates, expert_ids, slot_expert, w_in, w_out):
    members = lax.axis_size("ep")
    myself = lax.axis_index("ep")
    tok_rows, width = tokens.shape
    top_count = expert_ids.shape[1]
    experts = members // GROUP
    cap_expert = min(tok_rows, 5 * tok_rows * top_count // (4 * experts))
    cap_member = (cap_expert + GROUP - 1) // GROUP
    slot_total = members * cap_member
    block_limit = slot_total // BLOCK + 1
    expert_range = jnp.arange(experts, dtype=jnp.int32)
    home = jnp.sum(
        jnp.where(slot_expert[:, None] == expert_range[None, :], expert_range[:, None], 0), axis=0
    )
    pieces_in, pieces_out = (w_in, w_out)
    bit_order = (0, 1)
    for swap_bit in bit_order:
        other_in, other_out = from_partner((pieces_in, pieces_out), "ep", swap_bit)
        lower = myself // (1 << swap_bit) % 2 == 0
        pieces_in = jnp.where(
            lower,
            jnp.concatenate([pieces_in, other_in], axis=0),
            jnp.concatenate([other_in, pieces_in], axis=0),
        )
        pieces_out = jnp.where(
            lower,
            jnp.concatenate([pieces_out, other_out], axis=0),
            jnp.concatenate([other_out, pieces_out], axis=0),
        )
    flat_ids = expert_ids.reshape(-1)
    onehot = (flat_ids[:, None] == expert_range[None, :]).astype(jnp.int32)
    rank = jnp.sum(jnp.cumsum(onehot, axis=0) * onehot, axis=1) - 1
    group = jnp.sum(onehot * home[None, :], axis=1)
    member = rank // cap_member
    slot = rank % cap_member
    slot_index = (group * GROUP + member) * cap_member + slot
    repeated = jnp.repeat(tokens, top_count, axis=0)
    send_rows = jnp.zeros((slot_total, width), jnp.bfloat16).at[slot_index].set(repeated)
    send_flag = (
        jnp.zeros((slot_total,), jnp.bfloat16).at[slot_index].set(jnp.ones((), jnp.bfloat16))
    )
    recv_rows, recv_flag = (
        lax.all_to_all(send_rows, "ep", split_axis=0, concat_axis=0, tiled=True),
        lax.all_to_all(send_flag, "ep", split_axis=0, concat_axis=0, tiled=True),
    )
    valid = recv_flag > 0.5
    valid_count = jnp.sum(valid.astype(jnp.int32))
    blocks_total = (valid_count + BLOCK - 1) // BLOCK
    position = jnp.where(valid, jnp.cumsum(valid.astype(jnp.int32)) - 1, block_limit * BLOCK)
    compact = (
        jnp.zeros((block_limit * BLOCK, width), jnp.bfloat16)
        .at[position]
        .set(recv_rows, mode="drop")
    )
    gate_weights = pieces_in[:, 0]
    up_weights = pieces_in[:, 1]

    def compute_block(block, result):
        block_rows = lax.dynamic_slice_in_dim(compact, block * BLOCK, BLOCK, 0)
        gate_part = jnp.einsum(
            "rd,jfd->rjf", block_rows, gate_weights, preferred_element_type=jnp.float32
        )
        up_part = jnp.einsum(
            "rd,jfd->rjf", block_rows, up_weights, preferred_element_type=jnp.float32
        )
        hidden = (jax.nn.silu(gate_part) * up_part).astype(jnp.bfloat16)
        produced = jnp.einsum(
            "rjf,jfd->rd", hidden, pieces_out, preferred_element_type=jnp.float32
        ).astype(jnp.bfloat16)
        return lax.dynamic_update_slice_in_dim(result, produced, block * BLOCK, 0)

    computed = lax.fori_loop(
        0, blocks_total, compute_block, jnp.zeros((block_limit * BLOCK, width), jnp.bfloat16)
    )
    back_rows = jnp.where(
        valid[:, None],
        computed[jnp.minimum(position, block_limit * BLOCK - 1)],
        jnp.zeros((), jnp.bfloat16),
    )
    returned = lax.all_to_all(back_rows, "ep", split_axis=0, concat_axis=0, tiled=True)
    gathered = returned[slot_index].reshape(tok_rows, top_count, width)
    total = jnp.zeros((tok_rows, width), jnp.float32)
    for choice_index in range(top_count):
        total = total + gates[:, choice_index][:, None] * gathered[:, choice_index].astype(
            jnp.float32
        )
    return total.astype(jnp.bfloat16)


def local(tokens, gates, expert_ids, slot_expert, w_in, w_out):
    plan = everywhere if expert_ids.shape[1] == slot_expert.shape[0] == 2 else routed
    return plan(tokens, gates, expert_ids, slot_expert, w_in, w_out)


def solution(mesh):
    return jax.shard_map(
        local,
        mesh=mesh,
        in_specs=(
            P(("dp", "ep"), None),
            P(("dp", "ep"), None),
            P(("dp", "ep"), None),
            P("dp"),
            P(("dp", "ep"), None, None, None),
            P(("dp", "ep"), None, None),
        ),
        out_specs=P(("dp", "ep"), None),
        check_vma=False,
    )
```

```python
import jax
import jax.numpy as jnp
from jax import lax
from jax.experimental import pallas as pl
from jax.experimental.pallas import tpu as pltpu
from jax.sharding import PartitionSpec as P

GROUP = 4
BLOCK = 128


def from_partner(block, axis, apart):
    count = lax.axis_size(axis)
    route = []
    for low in range(count):
        high = low | 1 << apart
        if high != low and high < count:
            route += [(low, high), (high, low)]
    return lax.ppermute(block, axis, route)


def exchange(block, *apart):
    replicas, count = lax.axis_size("dp"), lax.axis_size("ep")
    route = []
    for d in range(replicas):
        bits = apart[d % len(apart)]
        route += [(i * replicas + d, (i ^ bits) * replicas + d) for i in range(count)]
    return lax.ppermute(block, ("ep", "dp"), route)


def after(value, *others):
    return lax.optimization_barrier((value, *others))[0]


def touch_kernel(w_in, w_out, out):
    out[...] = w_in[0, 0, :8, :128] + w_out[0, :8, :128]


def touch(w_in, w_out):
    return pl.pallas_call(
        touch_kernel,
        out_shape=jax.ShapeDtypeStruct((8, 128), jnp.bfloat16),
        in_specs=[pl.BlockSpec(memory_space=pltpu.VMEM)] * 2,
        out_specs=pl.BlockSpec(memory_space=pltpu.VMEM),
        compiler_params=pltpu.CompilerParams(has_side_effects=True),
        name="touch",
    )(w_in, w_out)


def share_kernel(*refs):
    n = (len(refs) - 2) // 2
    w_in, w_out = refs[n], refs[n + 1]
    rows = refs[0].shape[0]
    x = jnp.concatenate([r[...] for r in refs[:n]], axis=0)
    contract = (((1,), (1,)), ((), ()))
    gate = lax.dot_general(x, w_in[0, 0], contract, preferred_element_type=jnp.float32)
    up = lax.dot_general(x, w_in[0, 1], contract, preferred_element_type=jnp.float32)
    hidden = (gate / (1.0 + jnp.exp(-gate)) * up).astype(jnp.bfloat16)
    for i in range(n):
        refs[n + 2 + i][...] = jnp.dot(
            hidden[i * rows : (i + 1) * rows], w_out[0], preferred_element_type=jnp.float32
        ).astype(jnp.bfloat16)


def share(blocks, w_in, w_out):
    rows, width = blocks[0].shape
    units = w_out.shape[1]
    n = len(blocks)
    return pl.pallas_call(
        share_kernel,
        out_shape=[jax.ShapeDtypeStruct((rows, width), jnp.bfloat16)] * n,
        in_specs=[pl.BlockSpec(memory_space=pltpu.VMEM)] * (n + 2),
        out_specs=[pl.BlockSpec(memory_space=pltpu.VMEM)] * n,
        compiler_params=pltpu.CompilerParams(vmem_limit_bytes=32 << 20),
        cost_estimate=pl.CostEstimate(
            flops=6 * n * rows * width * units,
            bytes_accessed=2 * (2 * n * rows * width + 3 * units * width),
            transcendentals=n * rows * units,
        ),
        name="share",
    )(*blocks, w_in, w_out)


def summed(*shares):
    total = shares[0].astype(jnp.float32)
    for s in shares[1:]:
        total = total + s.astype(jnp.float32)
    return total.astype(jnp.bfloat16)


def everywhere(tokens, gates, expert_ids, slot_expert, w_in, w_out):
    first, second, across, group = (1, 2), (2, 1), (3, 3), (4, 4)
    my_group = lax.axis_index("ep") // GROUP
    weights = []
    for s in range(2):
        named = lax.dynamic_index_in_dim(slot_expert, (my_group + s) % 2, 0, keepdims=False)
        weights.append(jnp.sum(jnp.where(expert_ids == named, gates, 0.0), axis=1, keepdims=True))
    theirs = exchange(tokens, *group)
    ours_a = exchange(tokens, *first)
    ours_b = exchange(tokens, *second)
    ours_d = exchange(ours_a, *second)
    theirs = after(theirs, touch(w_in, w_out), ours_b)
    theirs_d = exchange(theirs, *across)
    theirs = after(theirs, ours_d)
    theirs_a = exchange(theirs, *first)
    theirs_b = exchange(theirs, *second)
    (away_d,) = share([theirs_d], w_in, w_out)
    away, away_a, away_b = share([theirs, theirs_a, theirs_b], w_in, w_out)
    back_a = exchange(away_a, *first)
    back_b = exchange(away_b, *second)
    back_d = exchange(away_d, *across)
    away_sum = summed(away, back_a, back_b, back_d)
    home = share([after(tokens, back_d), ours_a, ours_b, ours_d], w_in, w_out)
    home = [after(h, back_d) for h in home]
    home_d = exchange(home[3], *first)
    home_a = exchange(home[1], *first)
    home_b = exchange(summed(home[2], home_d), *second)
    other = exchange(away_sum, *group)
    own = summed(home[0], home_a, home_b)
    return (
        weights[0] * own.astype(jnp.float32) + weights[1] * other.astype(jnp.float32)
    ).astype(jnp.bfloat16)


def routed(tokens, gates, expert_ids, slot_expert, w_in, w_out):
    members = lax.axis_size("ep")
    myself = lax.axis_index("ep")
    tok_rows, width = tokens.shape
    top_count = expert_ids.shape[1]
    experts = members // GROUP
    cap_expert = min(tok_rows, 5 * tok_rows * top_count // (4 * experts))
    cap_member = (cap_expert + GROUP - 1) // GROUP
    slot_total = members * cap_member
    block_limit = slot_total // BLOCK + 1
    expert_range = jnp.arange(experts, dtype=jnp.int32)
    home = jnp.sum(
        jnp.where(slot_expert[:, None] == expert_range[None, :], expert_range[:, None], 0), axis=0
    )
    pieces_in, pieces_out = (w_in, w_out)
    bit_order = (0, 1)
    for swap_bit in bit_order:
        other_in, other_out = from_partner((pieces_in, pieces_out), "ep", swap_bit)
        lower = myself // (1 << swap_bit) % 2 == 0
        pieces_in = jnp.where(
            lower,
            jnp.concatenate([pieces_in, other_in], axis=0),
            jnp.concatenate([other_in, pieces_in], axis=0),
        )
        pieces_out = jnp.where(
            lower,
            jnp.concatenate([pieces_out, other_out], axis=0),
            jnp.concatenate([other_out, pieces_out], axis=0),
        )
    flat_ids = expert_ids.reshape(-1)
    onehot = (flat_ids[:, None] == expert_range[None, :]).astype(jnp.int32)
    rank = jnp.sum(jnp.cumsum(onehot, axis=0) * onehot, axis=1) - 1
    group = jnp.sum(onehot * home[None, :], axis=1)
    member = rank // cap_member
    slot = rank % cap_member
    slot_index = (group * GROUP + member) * cap_member + slot
    repeated = jnp.repeat(tokens, top_count, axis=0)
    send_rows = jnp.zeros((slot_total, width), jnp.bfloat16).at[slot_index].set(repeated)
    send_flag = (
        jnp.zeros((slot_total,), jnp.bfloat16).at[slot_index].set(jnp.ones((), jnp.bfloat16))
    )
    recv_rows, recv_flag = (
        lax.all_to_all(send_rows, "ep", split_axis=0, concat_axis=0, tiled=True),
        lax.all_to_all(send_flag, "ep", split_axis=0, concat_axis=0, tiled=True),
    )
    valid = recv_flag > 0.5
    valid_count = jnp.sum(valid.astype(jnp.int32))
    blocks_total = (valid_count + BLOCK - 1) // BLOCK
    position = jnp.where(valid, jnp.cumsum(valid.astype(jnp.int32)) - 1, block_limit * BLOCK)
    compact = (
        jnp.zeros((block_limit * BLOCK, width), jnp.bfloat16)
        .at[position]
        .set(recv_rows, mode="drop")
    )
    gate_weights = pieces_in[:, 0]
    up_weights = pieces_in[:, 1]

    def compute_block(block, result):
        block_rows = lax.dynamic_slice_in_dim(compact, block * BLOCK, BLOCK, 0)
        gate_part = jnp.einsum(
            "rd,jfd->rjf", block_rows, gate_weights, preferred_element_type=jnp.float32
        )
        up_part = jnp.einsum(
            "rd,jfd->rjf", block_rows, up_weights, preferred_element_type=jnp.float32
        )
        hidden = (jax.nn.silu(gate_part) * up_part).astype(jnp.bfloat16)
        produced = jnp.einsum(
            "rjf,jfd->rd", hidden, pieces_out, preferred_element_type=jnp.float32
        ).astype(jnp.bfloat16)
        return lax.dynamic_update_slice_in_dim(result, produced, block * BLOCK, 0)

    computed = lax.fori_loop(
        0, blocks_total, compute_block, jnp.zeros((block_limit * BLOCK, width), jnp.bfloat16)
    )
    back_rows = jnp.where(
        valid[:, None],
        computed[jnp.minimum(position, block_limit * BLOCK - 1)],
        jnp.zeros((), jnp.bfloat16),
    )
    returned = lax.all_to_all(back_rows, "ep", split_axis=0, concat_axis=0, tiled=True)
    gathered = returned[slot_index].reshape(tok_rows, top_count, width)
    total = jnp.zeros((tok_rows, width), jnp.float32)
    for choice_index in range(top_count):
        total = total + gates[:, choice_index][:, None] * gathered[:, choice_index].astype(
            jnp.float32
        )
    return total.astype(jnp.bfloat16)


def local(tokens, gates, expert_ids, slot_expert, w_in, w_out):
    plan = everywhere if expert_ids.shape[1] == slot_expert.shape[0] == 2 else routed
    return plan(tokens, gates, expert_ids, slot_expert, w_in, w_out)


def solution(mesh):
    return jax.shard_map(
        local,
        mesh=mesh,
        in_specs=(
            P(("dp", "ep"), None),
            P(("dp", "ep"), None),
            P(("dp", "ep"), None),
            P("dp"),
            P(("dp", "ep"), None, None, None),
            P(("dp", "ep"), None, None),
        ),
        out_specs=P(("dp", "ep"), None),
        check_vma=False,
    )
```

```python
import jax
import jax.numpy as jnp
from jax import lax
from jax.experimental import pallas as pl
from jax.experimental.pallas import tpu as pltpu
from jax.sharding import PartitionSpec as P

GROUP = 4
BLOCK = 128


def from_partner(block, axis, apart):
    count = lax.axis_size(axis)
    route = []
    for low in range(count):
        high = low | 1 << apart
        if high != low and high < count:
            route += [(low, high), (high, low)]
    return lax.ppermute(block, axis, route)


def exchange(block, *apart):
    replicas, count = lax.axis_size("dp"), lax.axis_size("ep")
    route = []
    for d in range(replicas):
        bits = apart[d % len(apart)]
        route += [(i * replicas + d, (i ^ bits) * replicas + d) for i in range(count)]
    return lax.ppermute(block, ("ep", "dp"), route)


def after(value, *others):
    return lax.optimization_barrier((value, *others))[0]


def touch_kernel(w_in, w_out, out):
    out[...] = w_in[0, 0, :8, :128] + w_out[0, :8, :128]


def touch(w_in, w_out):
    return pl.pallas_call(
        touch_kernel,
        out_shape=jax.ShapeDtypeStruct((8, 128), jnp.bfloat16),
        in_specs=[pl.BlockSpec(memory_space=pltpu.VMEM)] * 2,
        out_specs=pl.BlockSpec(memory_space=pltpu.VMEM),
        compiler_params=pltpu.CompilerParams(has_side_effects=True),
        name="touch",
    )(w_in, w_out)


def share_kernel(*refs):
    n = (len(refs) - 2) // 2
    w_in, w_out = refs[n], refs[n + 1]
    rows = refs[0].shape[0]
    x = jnp.concatenate([r[...] for r in refs[:n]], axis=0)
    contract = (((1,), (1,)), ((), ()))
    gate = lax.dot_general(x, w_in[0, 0], contract, preferred_element_type=jnp.float32)
    up = lax.dot_general(x, w_in[0, 1], contract, preferred_element_type=jnp.float32)
    hidden = (gate / (1.0 + jnp.exp(-gate)) * up).astype(jnp.bfloat16)
    for i in range(n):
        refs[n + 2 + i][...] = jnp.dot(
            hidden[i * rows : (i + 1) * rows], w_out[0], preferred_element_type=jnp.float32
        ).astype(jnp.bfloat16)


def share(blocks, w_in, w_out):
    rows, width = blocks[0].shape
    units = w_out.shape[1]
    n = len(blocks)
    return pl.pallas_call(
        share_kernel,
        out_shape=[pltpu.VMEM((rows, width), jnp.bfloat16)] * n,
        in_specs=[pl.BlockSpec(memory_space=pltpu.VMEM)] * (n + 2),
        out_specs=[pl.BlockSpec(memory_space=pltpu.VMEM)] * n,
        compiler_params=pltpu.CompilerParams(vmem_limit_bytes=32 << 20),
        cost_estimate=pl.CostEstimate(
            flops=6 * n * rows * width * units,
            bytes_accessed=2 * (2 * n * rows * width + 3 * units * width),
            transcendentals=n * rows * units,
        ),
        name="share",
    )(*blocks, w_in, w_out)


def summed(*shares):
    total = shares[0].astype(jnp.float32)
    for s in shares[1:]:
        total = total + s.astype(jnp.float32)
    return total.astype(jnp.bfloat16)


def everywhere(tokens, gates, expert_ids, slot_expert, w_in, w_out):
    first, second, across, group = (1, 2), (2, 1), (3, 3), (4, 4)
    my_group = lax.axis_index("ep") // GROUP
    weights = []
    for s in range(2):
        named = lax.dynamic_index_in_dim(slot_expert, (my_group + s) % 2, 0, keepdims=False)
        weights.append(jnp.sum(jnp.where(expert_ids == named, gates, 0.0), axis=1, keepdims=True))
    theirs = exchange(tokens, *group)
    ours_a = exchange(tokens, *first)
    ours_b = exchange(tokens, *second)
    ours_d = exchange(ours_a, *second)
    theirs = after(theirs, touch(w_in, w_out), ours_b)
    theirs_d = exchange(theirs, *across)
    theirs = after(theirs, ours_d)
    theirs_a = exchange(theirs, *first)
    theirs_b = exchange(theirs, *second)
    (away_d,) = share([theirs_d], w_in, w_out)
    away, away_a, away_b = share([theirs, theirs_a, theirs_b], w_in, w_out)
    back_d = exchange(away_d, *first)
    back_a = exchange(away_a, *first)
    back_b = exchange(summed(away_b, back_d), *second)
    away_sum = summed(away, back_a, back_b)
    home = share([after(tokens, back_d), ours_a, ours_b, ours_d], w_in, w_out)
    home = [after(h, back_d) for h in home]
    home_d = exchange(home[3], *second)
    home_b = exchange(home[2], *second)
    home_a = exchange(summed(home[1], home_d), *first)
    other = exchange(away_sum, *group)
    own = summed(home[0], home_a, home_b)
    return (
        weights[0] * own.astype(jnp.float32) + weights[1] * other.astype(jnp.float32)
    ).astype(jnp.bfloat16)


def routed(tokens, gates, expert_ids, slot_expert, w_in, w_out):
    members = lax.axis_size("ep")
    myself = lax.axis_index("ep")
    tok_rows, width = tokens.shape
    top_count = expert_ids.shape[1]
    experts = members // GROUP
    cap_expert = min(tok_rows, 5 * tok_rows * top_count // (4 * experts))
    cap_member = (cap_expert + GROUP - 1) // GROUP
    slot_total = members * cap_member
    block_limit = slot_total // BLOCK + 1
    expert_range = jnp.arange(experts, dtype=jnp.int32)
    home = jnp.sum(
        jnp.where(slot_expert[:, None] == expert_range[None, :], expert_range[:, None], 0), axis=0
    )
    pieces_in, pieces_out = (w_in, w_out)
    bit_order = (0, 1)
    for swap_bit in bit_order:
        other_in, other_out = from_partner((pieces_in, pieces_out), "ep", swap_bit)
        lower = myself // (1 << swap_bit) % 2 == 0
        pieces_in = jnp.where(
            lower,
            jnp.concatenate([pieces_in, other_in], axis=0),
            jnp.concatenate([other_in, pieces_in], axis=0),
        )
        pieces_out = jnp.where(
            lower,
            jnp.concatenate([pieces_out, other_out], axis=0),
            jnp.concatenate([other_out, pieces_out], axis=0),
        )
    flat_ids = expert_ids.reshape(-1)
    onehot = (flat_ids[:, None] == expert_range[None, :]).astype(jnp.int32)
    rank = jnp.sum(jnp.cumsum(onehot, axis=0) * onehot, axis=1) - 1
    group = jnp.sum(onehot * home[None, :], axis=1)
    member = rank // cap_member
    slot = rank % cap_member
    slot_index = (group * GROUP + member) * cap_member + slot
    repeated = jnp.repeat(tokens, top_count, axis=0)
    send_rows = jnp.zeros((slot_total, width), jnp.bfloat16).at[slot_index].set(repeated)
    send_flag = (
        jnp.zeros((slot_total,), jnp.bfloat16).at[slot_index].set(jnp.ones((), jnp.bfloat16))
    )
    recv_rows, recv_flag = (
        lax.all_to_all(send_rows, "ep", split_axis=0, concat_axis=0, tiled=True),
        lax.all_to_all(send_flag, "ep", split_axis=0, concat_axis=0, tiled=True),
    )
    valid = recv_flag > 0.5
    valid_count = jnp.sum(valid.astype(jnp.int32))
    blocks_total = (valid_count + BLOCK - 1) // BLOCK
    position = jnp.where(valid, jnp.cumsum(valid.astype(jnp.int32)) - 1, block_limit * BLOCK)
    compact = (
        jnp.zeros((block_limit * BLOCK, width), jnp.bfloat16)
        .at[position]
        .set(recv_rows, mode="drop")
    )
    gate_weights = pieces_in[:, 0]
    up_weights = pieces_in[:, 1]

    def compute_block(block, result):
        block_rows = lax.dynamic_slice_in_dim(compact, block * BLOCK, BLOCK, 0)
        gate_part = jnp.einsum(
            "rd,jfd->rjf", block_rows, gate_weights, preferred_element_type=jnp.float32
        )
        up_part = jnp.einsum(
            "rd,jfd->rjf", block_rows, up_weights, preferred_element_type=jnp.float32
        )
        hidden = (jax.nn.silu(gate_part) * up_part).astype(jnp.bfloat16)
        produced = jnp.einsum(
            "rjf,jfd->rd", hidden, pieces_out, preferred_element_type=jnp.float32
        ).astype(jnp.bfloat16)
        return lax.dynamic_update_slice_in_dim(result, produced, block * BLOCK, 0)

    computed = lax.fori_loop(
        0, blocks_total, compute_block, jnp.zeros((block_limit * BLOCK, width), jnp.bfloat16)
    )
    back_rows = jnp.where(
        valid[:, None],
        computed[jnp.minimum(position, block_limit * BLOCK - 1)],
        jnp.zeros((), jnp.bfloat16),
    )
    returned = lax.all_to_all(back_rows, "ep", split_axis=0, concat_axis=0, tiled=True)
    gathered = returned[slot_index].reshape(tok_rows, top_count, width)
    total = jnp.zeros((tok_rows, width), jnp.float32)
    for choice_index in range(top_count):
        total = total + gates[:, choice_index][:, None] * gathered[:, choice_index].astype(
            jnp.float32
        )
    return total.astype(jnp.bfloat16)


def local(tokens, gates, expert_ids, slot_expert, w_in, w_out):
    plan = everywhere if expert_ids.shape[1] == slot_expert.shape[0] == 2 else routed
    return plan(tokens, gates, expert_ids, slot_expert, w_in, w_out)


def solution(mesh):
    return jax.shard_map(
        local,
        mesh=mesh,
        in_specs=(
            P(("dp", "ep"), None),
            P(("dp", "ep"), None),
            P(("dp", "ep"), None),
            P("dp"),
            P(("dp", "ep"), None, None, None),
            P(("dp", "ep"), None, None),
        ),
        out_specs=P(("dp", "ep"), None),
        check_vma=False,
    )
```

```python
import jax
import jax.numpy as jnp
from jax import lax
from jax.experimental import pallas as pl
from jax.experimental.pallas import tpu as pltpu
from jax.sharding import PartitionSpec as P

GROUP = 4
BLOCK = 128


def from_partner(block, axis, apart):
    count = lax.axis_size(axis)
    route = []
    for low in range(count):
        high = low | 1 << apart
        if high != low and high < count:
            route += [(low, high), (high, low)]
    return lax.ppermute(block, axis, route)


def exchange(block, *apart):
    replicas, count = lax.axis_size("dp"), lax.axis_size("ep")
    route = []
    for d in range(replicas):
        bits = apart[d % len(apart)]
        route += [(i * replicas + d, (i ^ bits) * replicas + d) for i in range(count)]
    return lax.ppermute(block, ("ep", "dp"), route)


def after(value, *others):
    return lax.optimization_barrier((value, *others))[0]


def touch_kernel(w_in, w_out, out):
    out[...] = w_in[0, 0, :8, :128] + w_out[0, :8, :128]


def touch(w_in, w_out):
    return pl.pallas_call(
        touch_kernel,
        out_shape=jax.ShapeDtypeStruct((8, 128), jnp.bfloat16),
        in_specs=[pl.BlockSpec(memory_space=pltpu.VMEM)] * 2,
        out_specs=pl.BlockSpec(memory_space=pltpu.VMEM),
        compiler_params=pltpu.CompilerParams(has_side_effects=True),
        name="touch",
    )(w_in, w_out)


def share_kernel(*refs):
    n = (len(refs) - 2) // 2
    w_in, w_out = refs[n], refs[n + 1]
    rows = refs[0].shape[0]
    x = jnp.concatenate([r[...] for r in refs[:n]], axis=0)
    contract = (((1,), (1,)), ((), ()))
    gate = lax.dot_general(x, w_in[0, 0], contract, preferred_element_type=jnp.float32)
    up = lax.dot_general(x, w_in[0, 1], contract, preferred_element_type=jnp.float32)
    hidden = (gate / (1.0 + jnp.exp(-gate)) * up).astype(jnp.bfloat16)
    for i in range(n):
        refs[n + 2 + i][...] = jnp.dot(
            hidden[i * rows : (i + 1) * rows], w_out[0], preferred_element_type=jnp.float32
        ).astype(jnp.bfloat16)


def share(blocks, w_in, w_out, load=1):
    rows, width = blocks[0].shape
    units = w_out.shape[1]
    n = len(blocks)
    return pl.pallas_call(
        share_kernel,
        out_shape=[pltpu.VMEM((rows, width), jnp.bfloat16)] * n,
        in_specs=[pl.BlockSpec(memory_space=pltpu.VMEM)] * (n + 2),
        out_specs=[pl.BlockSpec(memory_space=pltpu.VMEM)] * n,
        compiler_params=pltpu.CompilerParams(vmem_limit_bytes=32 << 20),
        cost_estimate=pl.CostEstimate(
            flops=load * 6 * n * rows * width * units,
            bytes_accessed=2 * (2 * n * rows * width + 3 * units * width),
            transcendentals=n * rows * units,
        ),
        name="share",
    )(*blocks, w_in, w_out)


def summed(*shares):
    total = shares[0].astype(jnp.float32)
    for s in shares[1:]:
        total = total + s.astype(jnp.float32)
    return total.astype(jnp.bfloat16)


def everywhere(tokens, gates, expert_ids, slot_expert, w_in, w_out):
    first, second, across, group = (1, 2), (2, 1), (3, 3), (4, 4)
    my_group = lax.axis_index("ep") // GROUP
    weights = []
    for s in range(2):
        named = lax.dynamic_index_in_dim(slot_expert, (my_group + s) % 2, 0, keepdims=False)
        weights.append(jnp.sum(jnp.where(expert_ids == named, gates, 0.0), axis=1, keepdims=True))
    theirs = exchange(tokens, *group)
    ours_a = exchange(tokens, *first)
    ours_b = exchange(tokens, *second)
    ours_d = exchange(ours_a, *second)
    theirs = after(theirs, touch(w_in, w_out), ours_b)
    theirs_d = exchange(theirs, *across)
    theirs = after(theirs, ours_d)
    theirs_a = exchange(theirs, *first)
    theirs_b = exchange(theirs, *second)
    (away_d,) = share([theirs_d], w_in, w_out, load=8)
    away, away_a, away_b = share([theirs, theirs_a, theirs_b], w_in, w_out)
    back_d = exchange(away_d, *first)
    back_a = exchange(away_a, *first)
    back_b = exchange(summed(away_b, back_d), *second)
    away_sum = summed(away, back_a, back_b)
    home = share([after(tokens, back_d), ours_a, ours_b, ours_d], w_in, w_out)
    home = [after(h, back_d) for h in home]
    home_d = exchange(home[3], *second)
    home_b = exchange(home[2], *second)
    home_a = exchange(summed(home[1], home_d), *first)
    other = exchange(away_sum, *group)
    own = summed(home[0], home_a, home_b)
    return (
        weights[0] * own.astype(jnp.float32) + weights[1] * other.astype(jnp.float32)
    ).astype(jnp.bfloat16)


def routed(tokens, gates, expert_ids, slot_expert, w_in, w_out):
    members = lax.axis_size("ep")
    myself = lax.axis_index("ep")
    tok_rows, width = tokens.shape
    top_count = expert_ids.shape[1]
    experts = members // GROUP
    cap_expert = min(tok_rows, 5 * tok_rows * top_count // (4 * experts))
    cap_member = (cap_expert + GROUP - 1) // GROUP
    slot_total = members * cap_member
    block_limit = slot_total // BLOCK + 1
    expert_range = jnp.arange(experts, dtype=jnp.int32)
    home = jnp.sum(
        jnp.where(slot_expert[:, None] == expert_range[None, :], expert_range[:, None], 0), axis=0
    )
    pieces_in, pieces_out = (w_in, w_out)
    bit_order = (0, 1)
    for swap_bit in bit_order:
        other_in, other_out = from_partner((pieces_in, pieces_out), "ep", swap_bit)
        lower = myself // (1 << swap_bit) % 2 == 0
        pieces_in = jnp.where(
            lower,
            jnp.concatenate([pieces_in, other_in], axis=0),
            jnp.concatenate([other_in, pieces_in], axis=0),
        )
        pieces_out = jnp.where(
            lower,
            jnp.concatenate([pieces_out, other_out], axis=0),
            jnp.concatenate([other_out, pieces_out], axis=0),
        )
    flat_ids = expert_ids.reshape(-1)
    onehot = (flat_ids[:, None] == expert_range[None, :]).astype(jnp.int32)
    rank = jnp.sum(jnp.cumsum(onehot, axis=0) * onehot, axis=1) - 1
    group = jnp.sum(onehot * home[None, :], axis=1)
    member = rank // cap_member
    slot = rank % cap_member
    slot_index = (group * GROUP + member) * cap_member + slot
    repeated = jnp.repeat(tokens, top_count, axis=0)
    send_rows = jnp.zeros((slot_total, width), jnp.bfloat16).at[slot_index].set(repeated)
    send_flag = (
        jnp.zeros((slot_total,), jnp.bfloat16).at[slot_index].set(jnp.ones((), jnp.bfloat16))
    )
    recv_rows, recv_flag = (
        lax.all_to_all(send_rows, "ep", split_axis=0, concat_axis=0, tiled=True),
        lax.all_to_all(send_flag, "ep", split_axis=0, concat_axis=0, tiled=True),
    )
    valid = recv_flag > 0.5
    valid_count = jnp.sum(valid.astype(jnp.int32))
    blocks_total = (valid_count + BLOCK - 1) // BLOCK
    position = jnp.where(valid, jnp.cumsum(valid.astype(jnp.int32)) - 1, block_limit * BLOCK)
    compact = (
        jnp.zeros((block_limit * BLOCK, width), jnp.bfloat16)
        .at[position]
        .set(recv_rows, mode="drop")
    )
    gate_weights = pieces_in[:, 0]
    up_weights = pieces_in[:, 1]

    def compute_block(block, result):
        block_rows = lax.dynamic_slice_in_dim(compact, block * BLOCK, BLOCK, 0)
        gate_part = jnp.einsum(
            "rd,jfd->rjf", block_rows, gate_weights, preferred_element_type=jnp.float32
        )
        up_part = jnp.einsum(
            "rd,jfd->rjf", block_rows, up_weights, preferred_element_type=jnp.float32
        )
        hidden = (jax.nn.silu(gate_part) * up_part).astype(jnp.bfloat16)
        produced = jnp.einsum(
            "rjf,jfd->rd", hidden, pieces_out, preferred_element_type=jnp.float32
        ).astype(jnp.bfloat16)
        return lax.dynamic_update_slice_in_dim(result, produced, block * BLOCK, 0)

    computed = lax.fori_loop(
        0, blocks_total, compute_block, jnp.zeros((block_limit * BLOCK, width), jnp.bfloat16)
    )
    back_rows = jnp.where(
        valid[:, None],
        computed[jnp.minimum(position, block_limit * BLOCK - 1)],
        jnp.zeros((), jnp.bfloat16),
    )
    returned = lax.all_to_all(back_rows, "ep", split_axis=0, concat_axis=0, tiled=True)
    gathered = returned[slot_index].reshape(tok_rows, top_count, width)
    total = jnp.zeros((tok_rows, width), jnp.float32)
    for choice_index in range(top_count):
        total = total + gates[:, choice_index][:, None] * gathered[:, choice_index].astype(
            jnp.float32
        )
    return total.astype(jnp.bfloat16)


def local(tokens, gates, expert_ids, slot_expert, w_in, w_out):
    plan = everywhere if expert_ids.shape[1] == slot_expert.shape[0] == 2 else routed
    return plan(tokens, gates, expert_ids, slot_expert, w_in, w_out)


def solution(mesh):
    return jax.shard_map(
        local,
        mesh=mesh,
        in_specs=(
            P(("dp", "ep"), None),
            P(("dp", "ep"), None),
            P(("dp", "ep"), None),
            P("dp"),
            P(("dp", "ep"), None, None, None),
            P(("dp", "ep"), None, None),
        ),
        out_specs=P(("dp", "ep"), None),
        check_vma=False,
    )
```

```python
import jax
import jax.numpy as jnp
from jax import lax
from jax.experimental import pallas as pl
from jax.experimental.pallas import tpu as pltpu
from jax.sharding import PartitionSpec as P

GROUP = 4
BLOCK = 128


def from_partner(block, axis, apart):
    count = lax.axis_size(axis)
    route = []
    for low in range(count):
        high = low | 1 << apart
        if high != low and high < count:
            route += [(low, high), (high, low)]
    return lax.ppermute(block, axis, route)


def exchange(block, *apart):
    replicas, count = lax.axis_size("dp"), lax.axis_size("ep")
    route = []
    for d in range(replicas):
        bits = apart[d % len(apart)]
        route += [(i * replicas + d, (i ^ bits) * replicas + d) for i in range(count)]
    return lax.ppermute(block, ("ep", "dp"), route)


def after(value, *others):
    return lax.optimization_barrier((value, *others))[0]


def touch_kernel(w_in, w_out, out):
    out[...] = w_in[0, 0, :8, :128] + w_out[0, :8, :128]


def touch(w_in, w_out):
    return pl.pallas_call(
        touch_kernel,
        out_shape=jax.ShapeDtypeStruct((8, 128), jnp.bfloat16),
        in_specs=[pl.BlockSpec(memory_space=pltpu.VMEM)] * 2,
        out_specs=pl.BlockSpec(memory_space=pltpu.VMEM),
        compiler_params=pltpu.CompilerParams(has_side_effects=True),
        name="touch",
    )(w_in, w_out)


def share_kernel(*refs):
    n = (len(refs) - 2) // 2
    w_in, w_out = refs[n], refs[n + 1]
    rows = refs[0].shape[0]
    x = jnp.concatenate([r[...] for r in refs[:n]], axis=0)
    contract = (((1,), (1,)), ((), ()))
    gate = lax.dot_general(x, w_in[0, 0], contract, preferred_element_type=jnp.float32)
    up = lax.dot_general(x, w_in[0, 1], contract, preferred_element_type=jnp.float32)
    hidden = (gate / (1.0 + jnp.exp(-gate)) * up).astype(jnp.bfloat16)
    for i in range(n):
        refs[n + 2 + i][...] = jnp.dot(
            hidden[i * rows : (i + 1) * rows], w_out[0], preferred_element_type=jnp.float32
        ).astype(jnp.bfloat16)


def share(blocks, w_in, w_out, load=1):
    rows, width = blocks[0].shape
    units = w_out.shape[1]
    n = len(blocks)
    return pl.pallas_call(
        share_kernel,
        out_shape=[pltpu.VMEM((rows, width), jnp.bfloat16)] * n,
        in_specs=[pl.BlockSpec(memory_space=pltpu.VMEM)] * (n + 2),
        out_specs=[pl.BlockSpec(memory_space=pltpu.VMEM)] * n,
        compiler_params=pltpu.CompilerParams(vmem_limit_bytes=32 << 20),
        cost_estimate=pl.CostEstimate(
            flops=load * 6 * n * rows * width * units,
            bytes_accessed=2 * (2 * n * rows * width + 3 * units * width),
            transcendentals=n * rows * units,
        ),
        name="share",
    )(*blocks, w_in, w_out)


def summed(*shares):
    total = shares[0].astype(jnp.float32)
    for s in shares[1:]:
        total = total + s.astype(jnp.float32)
    return total.astype(jnp.bfloat16)


def everywhere(tokens, gates, expert_ids, slot_expert, w_in, w_out):
    first, second, across, group = (1, 2), (2, 1), (3, 3), (4, 4)
    my_group = lax.axis_index("ep") // GROUP
    weights = []
    for s in range(2):
        named = lax.dynamic_index_in_dim(slot_expert, (my_group + s) % 2, 0, keepdims=False)
        weights.append(jnp.sum(jnp.where(expert_ids == named, gates, 0.0), axis=1, keepdims=True))
    theirs = exchange(tokens, *group)
    ours_a = exchange(tokens, *first)
    ours_b = exchange(tokens, *second)
    ours_d = exchange(ours_a, *second)
    theirs = after(theirs, touch(w_in, w_out), ours_a, ours_b)
    theirs_d = exchange(theirs, *across)
    theirs = after(theirs, ours_d)
    theirs_a = exchange(theirs, *first)
    theirs_b = exchange(theirs, *second)
    (away_d,) = share([theirs_d], w_in, w_out, load=16)
    away, away_a, away_b = share([theirs, theirs_a, theirs_b], w_in, w_out, load=4)
    back_d = exchange(away_d, *first)
    back_a = exchange(away_a, *first)
    back_b = exchange(summed(away_b, back_d), *second)
    away_sum = summed(away, back_a, back_b)
    home = share([tokens, ours_a, ours_b, ours_d], w_in, w_out, load=8)
    home = [after(h, back_d) for h in home]
    home_d = exchange(home[3], *second)
    home_b = exchange(home[2], *second)
    home_a = exchange(summed(home[1], home_d), *first)
    other = exchange(away_sum, *group)
    own = summed(home[0], home_a, home_b)
    return (
        weights[0] * own.astype(jnp.float32) + weights[1] * other.astype(jnp.float32)
    ).astype(jnp.bfloat16)


def routed(tokens, gates, expert_ids, slot_expert, w_in, w_out):
    members = lax.axis_size("ep")
    myself = lax.axis_index("ep")
    tok_rows, width = tokens.shape
    top_count = expert_ids.shape[1]
    experts = members // GROUP
    cap_expert = min(tok_rows, 5 * tok_rows * top_count // (4 * experts))
    cap_member = (cap_expert + GROUP - 1) // GROUP
    slot_total = members * cap_member
    block_limit = slot_total // BLOCK + 1
    expert_range = jnp.arange(experts, dtype=jnp.int32)
    home = jnp.sum(
        jnp.where(slot_expert[:, None] == expert_range[None, :], expert_range[:, None], 0), axis=0
    )
    pieces_in, pieces_out = (w_in, w_out)
    bit_order = (0, 1)
    for swap_bit in bit_order:
        other_in, other_out = from_partner((pieces_in, pieces_out), "ep", swap_bit)
        lower = myself // (1 << swap_bit) % 2 == 0
        pieces_in = jnp.where(
            lower,
            jnp.concatenate([pieces_in, other_in], axis=0),
            jnp.concatenate([other_in, pieces_in], axis=0),
        )
        pieces_out = jnp.where(
            lower,
            jnp.concatenate([pieces_out, other_out], axis=0),
            jnp.concatenate([other_out, pieces_out], axis=0),
        )
    flat_ids = expert_ids.reshape(-1)
    onehot = (flat_ids[:, None] == expert_range[None, :]).astype(jnp.int32)
    rank = jnp.sum(jnp.cumsum(onehot, axis=0) * onehot, axis=1) - 1
    group = jnp.sum(onehot * home[None, :], axis=1)
    member = rank // cap_member
    slot = rank % cap_member
    slot_index = (group * GROUP + member) * cap_member + slot
    repeated = jnp.repeat(tokens, top_count, axis=0)
    send_rows = jnp.zeros((slot_total, width), jnp.bfloat16).at[slot_index].set(repeated)
    send_flag = (
        jnp.zeros((slot_total,), jnp.bfloat16).at[slot_index].set(jnp.ones((), jnp.bfloat16))
    )
    recv_rows, recv_flag = (
        lax.all_to_all(send_rows, "ep", split_axis=0, concat_axis=0, tiled=True),
        lax.all_to_all(send_flag, "ep", split_axis=0, concat_axis=0, tiled=True),
    )
    valid = recv_flag > 0.5
    valid_count = jnp.sum(valid.astype(jnp.int32))
    blocks_total = (valid_count + BLOCK - 1) // BLOCK
    position = jnp.where(valid, jnp.cumsum(valid.astype(jnp.int32)) - 1, block_limit * BLOCK)
    compact = (
        jnp.zeros((block_limit * BLOCK, width), jnp.bfloat16)
        .at[position]
        .set(recv_rows, mode="drop")
    )
    gate_weights = pieces_in[:, 0]
    up_weights = pieces_in[:, 1]

    def compute_block(block, result):
        block_rows = lax.dynamic_slice_in_dim(compact, block * BLOCK, BLOCK, 0)
        gate_part = jnp.einsum(
            "rd,jfd->rjf", block_rows, gate_weights, preferred_element_type=jnp.float32
        )
        up_part = jnp.einsum(
            "rd,jfd->rjf", block_rows, up_weights, preferred_element_type=jnp.float32
        )
        hidden = (jax.nn.silu(gate_part) * up_part).astype(jnp.bfloat16)
        produced = jnp.einsum(
            "rjf,jfd->rd", hidden, pieces_out, preferred_element_type=jnp.float32
        ).astype(jnp.bfloat16)
        return lax.dynamic_update_slice_in_dim(result, produced, block * BLOCK, 0)

    computed = lax.fori_loop(
        0, blocks_total, compute_block, jnp.zeros((block_limit * BLOCK, width), jnp.bfloat16)
    )
    back_rows = jnp.where(
        valid[:, None],
        computed[jnp.minimum(position, block_limit * BLOCK - 1)],
        jnp.zeros((), jnp.bfloat16),
    )
    returned = lax.all_to_all(back_rows, "ep", split_axis=0, concat_axis=0, tiled=True)
    gathered = returned[slot_index].reshape(tok_rows, top_count, width)
    total = jnp.zeros((tok_rows, width), jnp.float32)
    for choice_index in range(top_count):
        total = total + gates[:, choice_index][:, None] * gathered[:, choice_index].astype(
            jnp.float32
        )
    return total.astype(jnp.bfloat16)


def local(tokens, gates, expert_ids, slot_expert, w_in, w_out):
    plan = everywhere if expert_ids.shape[1] == slot_expert.shape[0] == 2 else routed
    return plan(tokens, gates, expert_ids, slot_expert, w_in, w_out)


def solution(mesh):
    return jax.shard_map(
        local,
        mesh=mesh,
        in_specs=(
            P(("dp", "ep"), None),
            P(("dp", "ep"), None),
            P(("dp", "ep"), None),
            P("dp"),
            P(("dp", "ep"), None, None, None),
            P(("dp", "ep"), None, None),
        ),
        out_specs=P(("dp", "ep"), None),
        check_vma=False,
    )
```

```python
import jax
import jax.numpy as jnp
from jax import lax
from jax.experimental import pallas as pl
from jax.experimental.pallas import tpu as pltpu
from jax.sharding import PartitionSpec as P

GROUP = 4
BLOCK = 128


def from_partner(block, axis, apart):
    count = lax.axis_size(axis)
    route = []
    for low in range(count):
        high = low | 1 << apart
        if high != low and high < count:
            route += [(low, high), (high, low)]
    return lax.ppermute(block, axis, route)


def exchange(block, *apart):
    replicas, count = lax.axis_size("dp"), lax.axis_size("ep")
    route = []
    for d in range(replicas):
        bits = apart[d % len(apart)]
        route += [(i * replicas + d, (i ^ bits) * replicas + d) for i in range(count)]
    return lax.ppermute(block, ("ep", "dp"), route)


def after(value, *others):
    return lax.optimization_barrier((value, *others))[0]


def touch_kernel(w_in, w_out, out):
    out[...] = w_in[0, 0, :8, :128] + w_out[0, :8, :128]


def touch(w_in, w_out):
    return pl.pallas_call(
        touch_kernel,
        out_shape=jax.ShapeDtypeStruct((8, 128), jnp.bfloat16),
        in_specs=[pl.BlockSpec(memory_space=pltpu.VMEM)] * 2,
        out_specs=pl.BlockSpec(memory_space=pltpu.VMEM),
        compiler_params=pltpu.CompilerParams(has_side_effects=True),
        name="touch",
    )(w_in, w_out)


def share_kernel(*refs):
    n = (len(refs) - 2) // 2
    w_in, w_out = refs[n], refs[n + 1]
    rows = refs[0].shape[0]
    x = jnp.concatenate([r[...] for r in refs[:n]], axis=0)
    contract = (((1,), (1,)), ((), ()))
    gate = lax.dot_general(x, w_in[0, 0], contract, preferred_element_type=jnp.float32)
    up = lax.dot_general(x, w_in[0, 1], contract, preferred_element_type=jnp.float32)
    hidden = (gate / (1.0 + jnp.exp(-gate)) * up).astype(jnp.bfloat16)
    for i in range(n):
        refs[n + 2 + i][...] = jnp.dot(
            hidden[i * rows : (i + 1) * rows], w_out[0], preferred_element_type=jnp.float32
        ).astype(jnp.bfloat16)


def share(blocks, w_in, w_out, load=1):
    rows, width = blocks[0].shape
    units = w_out.shape[1]
    n = len(blocks)
    return pl.pallas_call(
        share_kernel,
        out_shape=[pltpu.VMEM((rows, width), jnp.bfloat16)] * n,
        in_specs=[pl.BlockSpec(memory_space=pltpu.VMEM)] * (n + 2),
        out_specs=[pl.BlockSpec(memory_space=pltpu.VMEM)] * n,
        compiler_params=pltpu.CompilerParams(vmem_limit_bytes=32 << 20),
        cost_estimate=pl.CostEstimate(
            flops=load * 6 * n * rows * width * units,
            bytes_accessed=2 * (2 * n * rows * width + 3 * units * width),
            transcendentals=n * rows * units,
        ),
        name="share",
    )(*blocks, w_in, w_out)


def summed(*shares):
    total = shares[0].astype(jnp.float32)
    for s in shares[1:]:
        total = total + s.astype(jnp.float32)
    return total.astype(jnp.bfloat16)


def everywhere(tokens, gates, expert_ids, slot_expert, w_in, w_out):
    first, second, across, group = (1, 2), (2, 1), (3, 3), (4, 4)
    my_group = lax.axis_index("ep") // GROUP
    weights = []
    for s in range(2):
        named = lax.dynamic_index_in_dim(slot_expert, (my_group + s) % 2, 0, keepdims=False)
        weights.append(jnp.sum(jnp.where(expert_ids == named, gates, 0.0), axis=1, keepdims=True))
    theirs = exchange(tokens, *group)
    ours_a = exchange(tokens, *first)
    ours_b = exchange(tokens, *second)
    ours_d = exchange(ours_a, *second)
    theirs = after(theirs, touch(w_in, w_out), ours_a, ours_b)
    theirs_d = exchange(theirs, *across)
    theirs = after(theirs, ours_d)
    theirs_a = exchange(theirs, *first)
    theirs_b = exchange(theirs, *second)
    (away_d,) = share([theirs_d], w_in, w_out, load=16)
    away, away_a, away_b = share([theirs, theirs_a, theirs_b], w_in, w_out, load=4)
    back_d = exchange(away_d, *first)
    back_a = exchange(away_a, *first)
    back_b = exchange(summed(away_b, back_d), *second)
    away_sum = summed(away, back_a, back_b)
    home = share([tokens, ours_a, ours_b, ours_d], w_in, w_out, load=8)
    home = [after(h, back_d) for h in home]
    both = exchange(jnp.concatenate([home[3], home[2]]), *second)
    home_d, home_b = jnp.split(both, 2)
    home_a = exchange(summed(home[1], home_d), *first)
    other = exchange(away_sum, *group)
    own = summed(home[0], home_a, home_b)
    return (
        weights[0] * own.astype(jnp.float32) + weights[1] * other.astype(jnp.float32)
    ).astype(jnp.bfloat16)


def routed(tokens, gates, expert_ids, slot_expert, w_in, w_out):
    members = lax.axis_size("ep")
    myself = lax.axis_index("ep")
    tok_rows, width = tokens.shape
    top_count = expert_ids.shape[1]
    experts = members // GROUP
    cap_expert = min(tok_rows, 5 * tok_rows * top_count // (4 * experts))
    cap_member = (cap_expert + GROUP - 1) // GROUP
    slot_total = members * cap_member
    block_limit = slot_total // BLOCK + 1
    expert_range = jnp.arange(experts, dtype=jnp.int32)
    home = jnp.sum(
        jnp.where(slot_expert[:, None] == expert_range[None, :], expert_range[:, None], 0), axis=0
    )
    pieces_in, pieces_out = (w_in, w_out)
    bit_order = (0, 1)
    for swap_bit in bit_order:
        other_in, other_out = from_partner((pieces_in, pieces_out), "ep", swap_bit)
        lower = myself // (1 << swap_bit) % 2 == 0
        pieces_in = jnp.where(
            lower,
            jnp.concatenate([pieces_in, other_in], axis=0),
            jnp.concatenate([other_in, pieces_in], axis=0),
        )
        pieces_out = jnp.where(
            lower,
            jnp.concatenate([pieces_out, other_out], axis=0),
            jnp.concatenate([other_out, pieces_out], axis=0),
        )
    flat_ids = expert_ids.reshape(-1)
    onehot = (flat_ids[:, None] == expert_range[None, :]).astype(jnp.int32)
    rank = jnp.sum(jnp.cumsum(onehot, axis=0) * onehot, axis=1) - 1
    group = jnp.sum(onehot * home[None, :], axis=1)
    member = rank // cap_member
    slot = rank % cap_member
    slot_index = (group * GROUP + member) * cap_member + slot
    repeated = jnp.repeat(tokens, top_count, axis=0)
    send_rows = jnp.zeros((slot_total, width), jnp.bfloat16).at[slot_index].set(repeated)
    send_flag = (
        jnp.zeros((slot_total,), jnp.bfloat16).at[slot_index].set(jnp.ones((), jnp.bfloat16))
    )
    recv_rows, recv_flag = (
        lax.all_to_all(send_rows, "ep", split_axis=0, concat_axis=0, tiled=True),
        lax.all_to_all(send_flag, "ep", split_axis=0, concat_axis=0, tiled=True),
    )
    valid = recv_flag > 0.5
    valid_count = jnp.sum(valid.astype(jnp.int32))
    blocks_total = (valid_count + BLOCK - 1) // BLOCK
    position = jnp.where(valid, jnp.cumsum(valid.astype(jnp.int32)) - 1, block_limit * BLOCK)
    compact = (
        jnp.zeros((block_limit * BLOCK, width), jnp.bfloat16)
        .at[position]
        .set(recv_rows, mode="drop")
    )
    gate_weights = pieces_in[:, 0]
    up_weights = pieces_in[:, 1]

    def compute_block(block, result):
        block_rows = lax.dynamic_slice_in_dim(compact, block * BLOCK, BLOCK, 0)
        gate_part = jnp.einsum(
            "rd,jfd->rjf", block_rows, gate_weights, preferred_element_type=jnp.float32
        )
        up_part = jnp.einsum(
            "rd,jfd->rjf", block_rows, up_weights, preferred_element_type=jnp.float32
        )
        hidden = (jax.nn.silu(gate_part) * up_part).astype(jnp.bfloat16)
        produced = jnp.einsum(
            "rjf,jfd->rd", hidden, pieces_out, preferred_element_type=jnp.float32
        ).astype(jnp.bfloat16)
        return lax.dynamic_update_slice_in_dim(result, produced, block * BLOCK, 0)

    computed = lax.fori_loop(
        0, blocks_total, compute_block, jnp.zeros((block_limit * BLOCK, width), jnp.bfloat16)
    )
    back_rows = jnp.where(
        valid[:, None],
        computed[jnp.minimum(position, block_limit * BLOCK - 1)],
        jnp.zeros((), jnp.bfloat16),
    )
    returned = lax.all_to_all(back_rows, "ep", split_axis=0, concat_axis=0, tiled=True)
    gathered = returned[slot_index].reshape(tok_rows, top_count, width)
    total = jnp.zeros((tok_rows, width), jnp.float32)
    for choice_index in range(top_count):
        total = total + gates[:, choice_index][:, None] * gathered[:, choice_index].astype(
            jnp.float32
        )
    return total.astype(jnp.bfloat16)


def local(tokens, gates, expert_ids, slot_expert, w_in, w_out):
    plan = everywhere if expert_ids.shape[1] == slot_expert.shape[0] == 2 else routed
    return plan(tokens, gates, expert_ids, slot_expert, w_in, w_out)


def solution(mesh):
    return jax.shard_map(
        local,
        mesh=mesh,
        in_specs=(
            P(("dp", "ep"), None),
            P(("dp", "ep"), None),
            P(("dp", "ep"), None),
            P("dp"),
            P(("dp", "ep"), None, None, None),
            P(("dp", "ep"), None, None),
        ),
        out_specs=P(("dp", "ep"), None),
        check_vma=False,
    )
```
